512 devices in a mesh: section: 16 (over y, z_hi), dp: 32 (over z_lo, x, core).
Axes of the slice: x: 4, y: 4, z: 16 (z_hi: 4, z_lo: 4; z = z_hi * 4 + z_lo), core: 2. Of those that a mesh axis runs over, the one named last changes fastest.
Arguments:
- slab_store: bfloat16 [16, 32, 10, 16, 8192], P('section', 'dp'), may hold values from -600 to 600
- slab_place: int32 [16, 32, 8], P('section', 'dp'), may hold values from 0 to 19, as said below
- cotangent: bfloat16 [16, 32, 128, 8192], P('section', 'dp'), may hold values from -18 to 18
- norm_gain: bfloat16 [16, 8192], P('section'), may hold values from 0.099609375 to 1.8984375
Outputs:
- gain_grad: float32 [16, 8192], P('section')
- inner_prods: float32 [16, 32, 128], P('section', 'dp')
The draws below stay inside these ranges and needn't reach their ends.
Inputs may be any that keep to these rules, and one draw needn't show every extreme that they name: `slab_place`: A device's 8 entries are distinct. An entry v below 10 names slot v of the device's own store; an entry v of 10 or more names slot v - 10 of the store of the device with the same dp index on section 15 - s. No slot is named twice by the two devices of a mirrored pair. At most 4 entries of a device name the mirrored store, and some device has exactly 4.
All inputs are finite; a program needn't handle non-finite values.
Results may differ from the reference program's by a relative error of at most 0.0003.
Values may be sent and summed in bfloat16 or wider, within the bound.
No kernel may reach another device: no remote copies, remote signals or barrier semaphores. Data moves between devices by JAX's collectives and lax.ppermute only.
A program may use at most 64 MiB of HBM per device.

```python
import math
import jax
import jax.numpy as jnp
from jax import lax

D = 8192
SLAB = 16
SLABS = 8
SLOTS = 10
EVMAX = 4
TOK = 128
SECTIONS = 16
DPW = 32


def draw_slab_store(key, part):
    key = jax.random.fold_in(key, 11)
    keys = jax.random.split(key, 3)
    shape = (SECTIONS, DPW, SLOTS, SLAB, D)
    base = jnp.clip(jax.random.normal(keys[0], shape, jnp.float32), -6.0, 6.0)
    row_scale = jnp.exp(jax.random.uniform(keys[1], (SECTIONS, DPW, SLOTS, SLAB, 1), jnp.float32, 0.0, math.log(10.0)))
    col_scale = jnp.exp(jax.random.uniform(keys[2], (SECTIONS, 1, 1, 1, D), jnp.float32, 0.0, math.log(10.0)))
    return (base * row_scale * col_scale).astype(jnp.bfloat16)


def draw_cotangent(key, part):
    key = jax.random.fold_in(key, 23)
    shape = (SECTIONS, DPW, TOK, D)
    position = jnp.arange(DPW, dtype=jnp.float32).reshape(1, DPW, 1, 1) / max(DPW - 1, 1)
    base = jnp.clip(jax.random.normal(key, shape, jnp.float32), -6.0, 6.0)
    ramp = 1.0 + 2.0 * position
    return (base * ramp).astype(jnp.bfloat16)


def shuffled(key, lead, width):
    scores = jax.random.randint(key, lead + (width,), 0, 65536) * width + jnp.arange(width, dtype=jnp.int32)
    return jnp.argsort(scores, axis=-1).astype(jnp.int32)


def entries(home, away, out_home, out_away):
    lead = home.shape[:-1]
    steps = jnp.broadcast_to(jnp.arange(SLABS, dtype=jnp.int32), lead + (SLABS,))
    keep = SLABS - out_home[..., None]
    local = jnp.take_along_axis(home, jnp.clip(steps, 0, SLOTS - 1), axis=-1)
    offset = jnp.clip(SLABS - out_away[..., None] + steps - keep, 0, SLOTS - 1)
    remote = SLOTS + jnp.take_along_axis(away, offset, axis=-1)
    return jnp.where(steps < keep, local, remote).astype(jnp.int32)


def draw_slab_place(key, part):
    key = jax.random.fold_in(key, 37)
    keys = jax.random.split(key, 7)
    half = SECTIONS // 2
    early_out = jax.random.randint(keys[0], (half, DPW), 2, EVMAX + 1)
    chosen = jax.random.randint(keys[1], (), 0, half * DPW)
    flat = jnp.arange(half * DPW, dtype=jnp.int32).reshape(half, DPW)
    early_out = jnp.where(flat == chosen, EVMAX, early_out).astype(jnp.int32)
    late_out = jnp.clip(early_out - jax.random.randint(keys[2], (half, DPW), 0, 3), 0, EVMAX).astype(jnp.int32)
    perm_early = shuffled(keys[3], (half, DPW), SLOTS)
    perm_late = shuffled(keys[4], (half, DPW), SLOTS)
    early = entries(perm_early, perm_late, early_out, late_out)
    late = entries(perm_late, perm_early, late_out, early_out)
    early = jnp.take_along_axis(early, shuffled(keys[5], (half, DPW), SLABS), axis=-1)
    late = jnp.take_along_axis(late, shuffled(keys[6], (half, DPW), SLABS), axis=-1)
    return jnp.concatenate([early, late[::-1]], axis=0).astype(jnp.int32)


def setup_inputs(seed: int = 0) -> dict:
    key_list = jax.random.split(jax.random.key(seed), 5)
    return {
        "slab_store": draw_slab_store(jax.random.fold_in(key_list[4], 71), 0),
        "slab_place": draw_slab_place(jax.random.fold_in(key_list[4], 71), 0),
        "cotangent": draw_cotangent(jax.random.fold_in(key_list[4], 71), 0),
        "norm_gain": jnp.clip(1.0 + 0.18 * jax.random.normal(key_list[3], (SECTIONS, D), jnp.float32), 0.099609375, 1.8984375).astype(jnp.bfloat16),
    }


epsilon = 1e-05

def pick_slabs(combined, places):
    return jnp.take(combined, places, axis=0)

def reference(slab_store, slab_place, cotangent, norm_gain):

    def per_section(section_index):
        own_store = slab_store[section_index]
        mirror = slab_store[SECTIONS - 1 - section_index]
        combined = jnp.concatenate([own_store, mirror], axis=1)
        places = slab_place[section_index].astype(jnp.int32)
        gathered = jax.vmap(pick_slabs)(combined, places)
        tok_rows = gathered.reshape(DPW, SLABS * SLAB, D).astype(jnp.float32)
        inv_rms = lax.rsqrt(lax.optimization_barrier(jnp.mean(tok_rows * tok_rows, axis=-1, keepdims=True)) + epsilon)
        normed = tok_rows * inv_rms
        cotangents = cotangent[section_index].astype(jnp.float32)
        gain_part = lax.optimization_barrier(jnp.sum(cotangents * normed, axis=(0, 1))) / math.sqrt(DPW * SLABS * SLAB)
        gain_row = norm_gain[section_index].astype(jnp.float32)
        inner_part = lax.optimization_barrier(jnp.sum(normed * gain_row * cotangents, axis=-1)) / math.sqrt(D)
        return (gain_part, inner_part)
    gain_grad, inner_prods = lax.map(per_section, jnp.arange(SECTIONS, dtype=jnp.int32))
    return (gain_grad, inner_prods)
```

```python
import functools
import math

import jax
import jax.numpy as jnp
from jax import lax
from jax.experimental import pallas as pl
from jax.experimental.pallas import tpu as pltpu
from jax.sharding import PartitionSpec as P

epsilon = 1e-05
MOST = 4
LANES = 128
STEP = 512
SMEM = pl.BlockSpec(memory_space=pltpu.SMEM)
VMEM = pl.BlockSpec(memory_space=pltpu.VMEM)
HBM = pl.BlockSpec(memory_space=pl.ANY)
LIMIT = pltpu.CompilerParams(vmem_limit_bytes=24 * 1024 * 1024)


def mirror(array):
    size = lax.axis_size("section")
    return lax.ppermute(array, "section", [(i, size - 1 - i) for i in range(size)])


def nth_away(places, slots, n):
    seen = position = slot = found = jnp.int32(0)
    for k in range(places.shape[0]):
        place = places[k]
        away = (place >= slots).astype(jnp.int32)
        hit = away * (seen == n).astype(jnp.int32)
        position = position + hit * k
        slot = slot + hit * (place - slots)
        found = found + hit
        seen = seen + away
    return position, slot, found


def count_away(places, slots):
    return sum((places[k] >= slots).astype(jnp.int32) for k in range(places.shape[0]))


def fold(block):
    total = block[:, :LANES]
    for j in range(LANES, block.shape[1], LANES):
        total = total + block[:, j : j + LANES]
    return total


def slab_terms(x, c, g, grad):
    width = x.shape[1]
    squares = jnp.zeros((x.shape[0], LANES), jnp.float32)
    for j in range(0, width, STEP):
        rows = x[:, j : j + STEP].astype(jnp.float32)
        squares = squares + fold(rows * rows)
    inv_rms = lax.rsqrt(jnp.sum(squares, axis=1, keepdims=True) / width + epsilon)
    inner = jnp.zeros((x.shape[0], LANES), jnp.float32)
    for j in range(0, width, STEP):
        product = x[:, j : j + STEP].astype(jnp.float32) * inv_rms * c[:, j : j + STEP].astype(jnp.float32)
        grad[:, j : j + STEP] += product[:8] + product[8:]
        inner = inner + fold(product * g[:, j : j + STEP].astype(jnp.float32))
    return inner


def pack_kernel(groups, slots, places, far_places, array, most, *refs):
    outs, sems = refs[:-1], refs[-1]
    copies = []
    for out, numbers in zip(outs, groups):
        for i, n in enumerate(numbers):
            _, slot, _ = nth_away(far_places, slots, n)
            copies.append(pltpu.make_async_copy(array.at[slot], out.at[i], sems.at[len(copies)]))
            copies[-1].start()
    most[0] = jnp.maximum(count_away(places, slots), count_away(far_places, slots))
    for copy in copies:
        copy.wait()


def pack(places, far_places, store, groups):
    shapes = [jax.ShapeDtypeStruct((len(numbers),) + store.shape[1:], store.dtype) for numbers in groups]
    return pl.pallas_call(
        functools.partial(pack_kernel, groups, store.shape[0]),
        out_shape=[jax.ShapeDtypeStruct((1,), jnp.int32)] + shapes,
        in_specs=[SMEM, SMEM, HBM],
        out_specs=[SMEM] + [VMEM] * len(groups),
        scratch_shapes=[pltpu.SemaphoreType.DMA((sum(map(len, groups)),))],
        compiler_params=LIMIT,
    )(places, far_places, store)


def own_kernel(slots, places, x, c, g, grad, inner):
    step = pl.program_id(0)

    @pl.when(step == 0)
    def _():
        grad[...] = jnp.zeros_like(grad)

    here = places[step] < slots

    @pl.when(here)
    def _():
        inner[0] = slab_terms(x.at[0], c.at[0], g, grad)

    @pl.when(jnp.logical_not(here))
    def _():
        inner[...] = jnp.zeros_like(inner)


def own_terms(places, store, cotangents, gain):
    slots, slab, width = store.shape
    count = places.shape[0]
    return pl.pallas_call(
        functools.partial(own_kernel, slots),
        out_shape=(
            jax.ShapeDtypeStruct((8, width), jnp.float32),
            jax.ShapeDtypeStruct((count + 1, slab, LANES), jnp.float32),
        ),
        grid_spec=pltpu.PrefetchScalarGridSpec(
            num_scalar_prefetch=1,
            grid=(count,),
            in_specs=[
                pl.BlockSpec((1, slab, width), lambda i, places: (jnp.where(places[i] < slots, places[i], 0), 0, 0)),
                pl.BlockSpec((1, slab, width), lambda i, places: (i, 0, 0)),
                pl.BlockSpec((1, width), lambda i, places: (0, 0)),
            ],
            out_specs=[
                pl.BlockSpec((8, width), lambda i, places: (0, 0)),
                pl.BlockSpec((1, slab, LANES), lambda i, places: (i, 0, 0)),
            ],
        ),
        compiler_params=LIMIT,
    )(places, store, cotangents, gain)


def far_kernel(slots, first, places, x, c, g, grad_in, inner_in, grad, inner):
    step = pl.program_id(0)

    @pl.when(step == 0)
    def _():
        grad[...] = grad_in[...]

    @pl.when(nth_away(places, slots, step + first)[2] > 0)
    def _():
        inner[0] = slab_terms(x.at[0], c.at[0], g, grad)


def far_terms(places, slots, first, x, cotangents, gain, grad, inner):
    number, slab, width = x.shape
    spare = inner.shape[0] - 1

    def line(i, places):
        position, _, found = nth_away(places, slots, i + first)
        return jnp.where(found > 0, position, spare), 0, 0

    whole = pl.BlockSpec((8, width), lambda i, places: (0, 0))
    return pl.pallas_call(
        functools.partial(far_kernel, slots, first),
        out_shape=(jax.ShapeDtypeStruct(grad.shape, grad.dtype), jax.ShapeDtypeStruct(inner.shape, inner.dtype)),
        grid_spec=pltpu.PrefetchScalarGridSpec(
            num_scalar_prefetch=1,
            grid=(number,),
            in_specs=[
                pl.BlockSpec((1, slab, width), lambda i, places: (i, 0, 0)),
                pl.BlockSpec((1, slab, width), lambda i, places: (nth_away(places, slots, i + first)[0], 0, 0)),
                pl.BlockSpec((1, width), lambda i, places: (0, 0)),
                whole,
                HBM,
            ],
            out_specs=[whole, pl.BlockSpec((1, slab, LANES), line)],
        ),
        input_output_aliases={5: 1},
        compiler_params=LIMIT,
    )(places, x, cotangents, gain, grad, inner)


def sum_over_dp(row):
    size = lax.axis_size("dp")
    shares = lax.all_to_all(row.reshape(size, -1), "dp", 0, 0)
    share = jnp.sum(shares, axis=0)
    whole = lax.all_to_all(jnp.broadcast_to(share[None], (size,) + share.shape), "dp", 0, 0)
    return whole.reshape(-1)


def shards(slab_store, slab_place, cotangent, norm_gain):
    store = slab_store[0, 0]
    places = slab_place[0, 0]
    slots, slab, width = store.shape
    count = places.shape[0]
    cotangents = cotangent[0, 0].reshape(count, slab, width)

    far_places = mirror(places)
    most, *packs = pack(places, far_places, store, [range(n) for n in range(1, MOST + 1)])

    def exchange(number):
        def branch(packs, cotangents):
            grad, inner = own_terms(places, store, cotangents, norm_gain)
            if number:
                received = mirror(packs[number - 1])
                grad, inner = far_terms(places, slots, 0, received, cotangents, norm_gain, grad, inner)
            return grad, inner

        return branch

    grad, inner = lax.switch(most[0], [exchange(number) for number in range(MOST + 1)], packs, cotangents)

    tokens = lax.axis_size("dp") * count * slab
    gain_grad = sum_over_dp(jnp.sum(grad, axis=0)) / math.sqrt(tokens)
    inner_prods = jnp.sum(inner[:count], axis=-1).reshape(-1) / math.sqrt(width)
    return gain_grad[None, :], inner_prods[None, None, :]


def solution(mesh):
    placed = (
        P("section", "dp", None, None, None),
        P("section", "dp", None),
        P("section", "dp", None, None),
        P("section", None),
    )
    return jax.shard_map(
        shards,
        mesh=mesh,
        in_specs=placed,
        out_specs=(P("section", None), P("section", "dp", None)),
        check_vma=False,
    )
```

```python
import functools
import math

import jax
import jax.numpy as jnp
from jax import lax
from jax.experimental import pallas as pl
from jax.experimental.pallas import tpu as pltpu
from jax.sharding import PartitionSpec as P

epsilon = 1e-05
MOST = 4
LANES = 128
STEP = 512
SMEM = pl.BlockSpec(memory_space=pltpu.SMEM)
VMEM = pl.BlockSpec(memory_space=pltpu.VMEM)
HBM = pl.BlockSpec(memory_space=pl.ANY)
LIMIT = pltpu.CompilerParams(vmem_limit_bytes=24 * 1024 * 1024)


def mirror(array):
    size = lax.axis_size("section")
    return lax.ppermute(array, "section", [(i, size - 1 - i) for i in range(size)])


def nth_away(places, slots, n):
    seen = position = slot = found = jnp.int32(0)
    for k in range(places.shape[0]):
        place = places[k]
        away = (place >= slots).astype(jnp.int32)
        hit = away * (seen == n).astype(jnp.int32)
        position = position + hit * k
        slot = slot + hit * (place - slots)
        found = found + hit
        seen = seen + away
    return position, slot, found


def count_away(places, slots):
    return sum((places[k] >= slots).astype(jnp.int32) for k in range(places.shape[0]))


def fold(block):
    total = block[:, :LANES]
    for j in range(LANES, block.shape[1], LANES):
        total = total + block[:, j : j + LANES]
    return total


def slab_terms(x, c, g, grad):
    width = grad.shape[1]
    steps = [slice(j, j + STEP) for j in range(0, width, STEP)]
    squares = sum(fold(jnp.square(x(step))) for step in steps)
    inv_rms = lax.rsqrt(jnp.sum(squares, axis=1, keepdims=True) / width + epsilon)
    inner = jnp.zeros_like(squares)
    for step in steps:
        product = x(step) * inv_rms * c(step)
        grad[:, step] += product[:8] + product[8:] if product.shape[0] == 16 else product
        inner = inner + fold(product * g[:, step].astype(jnp.float32))
    return inner


def columns(ref, rows=slice(None)):
    return lambda step: ref[:, step].astype(jnp.float32)[rows]


def choose_kernel(slots, places, far_places, store, cotangents, branch, whole, half, sem):
    mine, theirs = count_away(places, slots), count_away(far_places, slots)
    more = jnp.abs(mine - theirs)
    branch[0] = 3 * jnp.minimum(mine, theirs) + more

    @pl.when(mine > theirs)
    def _():
        pltpu.make_async_copy(cotangents.at[nth_away(places, slots, mine - 1)[0]], whole, sem).start()

    @pl.when(mine <= theirs)
    def _():
        slot = nth_away(far_places, slots, theirs - jnp.maximum(more, 1))[1]
        pltpu.make_async_copy(store.at[slot], whole, sem).start()

    pltpu.make_async_copy(store.at[0], whole, sem).wait()
    for j in range(0, whole.shape[1], STEP):
        rows = whole[:, j : j + STEP].astype(jnp.float32)
        half[:, j : j + STEP] = jnp.where(mine > theirs, rows[8:], rows[:8]).astype(half.dtype)


def choose(places, far_places, store, cotangents):
    slab = jax.ShapeDtypeStruct(store.shape[1:], store.dtype)
    half = jax.ShapeDtypeStruct((8, store.shape[2]), store.dtype)
    return pl.pallas_call(
        functools.partial(choose_kernel, store.shape[0]),
        out_shape=[jax.ShapeDtypeStruct((1,), jnp.int32), slab, half],
        in_specs=[SMEM, SMEM, HBM, HBM],
        out_specs=[SMEM, VMEM, VMEM],
        scratch_shapes=[pltpu.SemaphoreType.DMA],
        compiler_params=LIMIT,
    )(places, far_places, store, cotangents)


def pack_kernel(slots, far_places, store, out, sems):
    copies = []
    for n in range(out.shape[0]):
        slot = nth_away(far_places, slots, n)[1]
        copies.append(pltpu.make_async_copy(store.at[slot], out.at[n], sems.at[n]))
        copies[-1].start()
    for copy in copies:
        copy.wait()


def pack(far_places, store, number):
    return pl.pallas_call(
        functools.partial(pack_kernel, store.shape[0]),
        out_shape=jax.ShapeDtypeStruct((number,) + store.shape[1:], store.dtype),
        in_specs=[SMEM, HBM],
        out_specs=VMEM,
        scratch_shapes=[pltpu.SemaphoreType.DMA((number,))],
        compiler_params=LIMIT,
    )(far_places, store)


def even_kernel(slots, more, places, far_places, y, x, c, g, far_g, grad_in, inner_in, grad, inner, back, back_grad):
    mine, theirs = count_away(places, slots), count_away(far_places, slots)
    width = grad.shape[1]
    grad[...] = grad_in[...]
    back[...] = jnp.zeros_like(back)
    given = columns(y)

    @pl.when(mine > theirs)
    def _():
        rows = slice(0, y.shape[0])
        inner[...] = jnp.zeros_like(inner)
        inner[0, rows] = slab_terms(given, columns(c.at[0], rows), g, grad)

    @pl.when(mine < theirs)
    def _():
        rows = slice(x.shape[1] - y.shape[0], None)
        back_grad[...] = jnp.zeros_like(back_grad)
        sums = jnp.sum(slab_terms(columns(x.at[0], rows), given, far_g, back_grad), axis=1, keepdims=True)
        token = lax.broadcasted_iota(jnp.int32, (y.shape[0], LANES), 0) + rows.start
        lane = lax.broadcasted_iota(jnp.int32, (y.shape[0], LANES), 1)
        back[:, width:] = jnp.sum(jnp.where(token == lane, sums, 0.0), axis=0, keepdims=True)
        for j in range(0, width, STEP):
            back[:, j : j + STEP] = jnp.sum(back_grad[:, j : j + STEP], axis=0, keepdims=True)


def even_terms(places, far_places, more, y, store, cotangents, gain, far_gain, grad, inner):
    slots, slab, width = store.shape
    spare = inner.shape[0] - 1

    def own_item(places, far_places):
        mine, theirs = count_away(places, slots), count_away(far_places, slots)
        return nth_away(places, slots, mine - more)[0], mine > theirs

    def far_item(i, places, far_places):
        return nth_away(far_places, slots, count_away(far_places, slots) - 1)[1], 0, 0

    def line(i, places, far_places):
        position, ours = own_item(places, far_places)
        return jnp.where(ours, position, spare), 0, 0

    def whole(*shape):
        return pl.BlockSpec(shape, lambda i, places, far_places: (0,) * len(shape))

    return pl.pallas_call(
        functools.partial(even_kernel, slots, more),
        out_shape=(
            jax.ShapeDtypeStruct(grad.shape, grad.dtype),
            jax.ShapeDtypeStruct(inner.shape, inner.dtype),
            jax.ShapeDtypeStruct((1, width + LANES), jnp.float32),
        ),
        grid_spec=pltpu.PrefetchScalarGridSpec(
            num_scalar_prefetch=2,
            grid=(1,),
            in_specs=[
                whole(*y.shape),
                pl.BlockSpec((1, slab, width), far_item),
                pl.BlockSpec((1, slab, width), lambda i, places, far_places: (own_item(places, far_places)[0], 0, 0)),
                whole(1, width),
                whole(1, width),
                whole(8, width),
                HBM,
            ],
            out_specs=[whole(8, width), pl.BlockSpec((1, slab, LANES), line), whole(1, width + LANES)],
            scratch_shapes=[pltpu.VMEM((8, width), jnp.float32)],
        ),
        cost_estimate=pl.CostEstimate(flops=4 * 10**10, bytes_accessed=10**6, transcendentals=0),
        input_output_aliases={8: 1},
        compiler_params=LIMIT,
    )(places, far_places, y, store, cotangents, gain, far_gain, grad, inner)


def own_kernel(slots, places, x, c, g, grad, inner):
    step = pl.program_id(0)

    @pl.when(step == 0)
    def _():
        grad[...] = jnp.zeros_like(grad)

    here = places[step] < slots

    @pl.when(here)
    def _():
        inner[0] = slab_terms(columns(x.at[0]), columns(c.at[0]), g, grad)

    @pl.when(jnp.logical_not(here))
    def _():
        inner[...] = jnp.zeros_like(inner)


def own_terms(places, store, cotangents, gain):
    slots, slab, width = store.shape
    count = places.shape[0]
    return pl.pallas_call(
        functools.partial(own_kernel, slots),
        out_shape=(
            jax.ShapeDtypeStruct((8, width), jnp.float32),
            jax.ShapeDtypeStruct((count + 1, slab, LANES), jnp.float32),
        ),
        grid_spec=pltpu.PrefetchScalarGridSpec(
            num_scalar_prefetch=1,
            grid=(count,),
            in_specs=[
                pl.BlockSpec((1, slab, width), lambda i, places: (jnp.where(places[i] < slots, places[i], 0), 0, 0)),
                pl.BlockSpec((1, slab, width), lambda i, places: (i, 0, 0)),
                pl.BlockSpec((1, width), lambda i, places: (0, 0)),
            ],
            out_specs=[
                pl.BlockSpec((8, width), lambda i, places: (0, 0)),
                pl.BlockSpec((1, slab, LANES), lambda i, places: (i, 0, 0)),
            ],
        ),
        compiler_params=LIMIT,
    )(places, store, cotangents, gain)


def write_row(grad, back, row):
    for j in range(0, row.shape[1], STEP):
        row[:, j : j + STEP] = jnp.sum(grad[:, j : j + STEP], axis=0, keepdims=True) + back[:, j : j + STEP]


def far_kernel(slots, places, x, c, g, grad_in, back, inner_in, row, inner, grad):
    step = pl.program_id(0)

    @pl.when(step == 0)
    def _():
        grad[...] = grad_in[...]

    inner[0] = slab_terms(columns(x.at[0]), columns(c.at[0]), g, grad)

    @pl.when(step == pl.num_programs(0) - 1)
    def _():
        write_row(grad, back, row)


def far_terms(places, slots, x, cotangents, gain, grad, back, inner):
    number, slab, width = x.shape

    def item(i, places):
        return nth_away(places, slots, i)[0], 0, 0

    def whole(*shape):
        return pl.BlockSpec(shape, lambda i, places: (0,) * len(shape))

    return pl.pallas_call(
        functools.partial(far_kernel, slots),
        out_shape=(jax.ShapeDtypeStruct((1, width), jnp.float32), jax.ShapeDtypeStruct(inner.shape, inner.dtype)),
        grid_spec=pltpu.PrefetchScalarGridSpec(
            num_scalar_prefetch=1,
            grid=(number,),
            in_specs=[
                pl.BlockSpec((1, slab, width), lambda i, places: (i, 0, 0)),
                pl.BlockSpec((1, slab, width), item),
                whole(1, width),
                whole(8, width),
                whole(1, width + LANES),
                HBM,
            ],
            out_specs=[whole(1, width), pl.BlockSpec((1, slab, LANES), item)],
            scratch_shapes=[pltpu.VMEM((8, width), jnp.float32)],
        ),
        input_output_aliases={6: 1},
        compiler_params=LIMIT,
    )(places, x, cotangents, gain, grad, back, inner)


def gradient_row(grad, back):
    return pl.pallas_call(
        write_row,
        out_shape=jax.ShapeDtypeStruct((1, grad.shape[1]), jnp.float32),
        in_specs=[VMEM, VMEM],
        out_specs=VMEM,
    )(grad, back)


def sum_over_dp(row):
    size = lax.axis_size("dp")
    shares = lax.all_to_all(row.reshape(size, -1), "dp", 0, 0)
    share = jnp.sum(shares, axis=0)
    whole = lax.all_to_all(jnp.broadcast_to(share[None], (size,) + share.shape), "dp", 0, 0)
    return whole.reshape(-1)


def shards(slab_store, slab_place, cotangent, norm_gain):
    store = slab_store[0, 0]
    places = slab_place[0, 0]
    slots, slab, width = store.shape
    count = places.shape[0]
    cotangents = cotangent[0, 0].reshape(count, slab, width)

    far_places = mirror(places)
    branch, whole, half = choose(places, far_places, store, cotangents)

    def exchange(fewer, more):
        def run(whole, half, cotangents):
            back = jnp.zeros((1, width + LANES), jnp.float32)
            if more:
                y = mirror(half if more == 1 else whole)
                far_gain = mirror(norm_gain)
            if fewer:
                received = mirror(pack(far_places, store, fewer))
            grad, inner = own_terms(places, store, cotangents, norm_gain)
            if more:
                grad, inner, back = even_terms(places, far_places, more, y, store, cotangents, norm_gain, far_gain, grad, inner)
                back = mirror(back)
            if fewer:
                row, inner = far_terms(places, slots, received, cotangents, norm_gain, grad, back, inner)
            else:
                row = gradient_row(grad, back)
            return row, inner, back[:, width : width + slab]

        return run

    branches = [exchange(fewer, more if fewer + more <= MOST else 0) for fewer in range(MOST + 1) for more in range(3)]
    row, inner, back = lax.switch(branch[0], branches[: 3 * MOST + 1], whole, half, cotangents)

    tokens = lax.axis_size("dp") * count * slab
    gain_grad = sum_over_dp(row[0]) / math.sqrt(tokens)
    places, row = lax.optimization_barrier((places, row))
    away = (places >= slots).astype(jnp.int32)
    last = (away > 0) & (jnp.cumsum(away) == jnp.sum(away))
    inner_prods = jnp.sum(inner[:count], axis=-1) + jnp.where(last[:, None], back, 0.0)
    inner_prods = inner_prods.reshape(-1) / math.sqrt(width)
    return gain_grad[None, :], inner_prods[None, None, :]


def solution(mesh):
    placed = (
        P("section", "dp", None, None, None),
        P("section", "dp", None),
        P("section", "dp", None, None),
        P("section", None),
    )
    return jax.shard_map(
        shards,
        mesh=mesh,
        in_specs=placed,
        out_specs=(P("section", None), P("section", "dp", None)),
        check_vma=False,
    )
```

```python
import functools
import math

import jax
import jax.numpy as jnp
from jax import lax
from jax.experimental import pallas as pl
from jax.experimental.pallas import tpu as pltpu
from jax.sharding import PartitionSpec as P

epsilon = 1e-05
MOST = 4
LANES = 128
STEP = 512
SMEM = pl.BlockSpec(memory_space=pltpu.SMEM)
VMEM = pl.BlockSpec(memory_space=pltpu.VMEM)
HBM = pl.BlockSpec(memory_space=pl.ANY)
LIMIT = pltpu.CompilerParams(vmem_limit_bytes=24 * 1024 * 1024)


def mirror(array):
    size = lax.axis_size("section")
    return lax.ppermute(array, "section", [(i, size - 1 - i) for i in range(size)])


def nth_away(places, slots, n):
    seen = position = slot = found = jnp.int32(0)
    for k in range(places.shape[0]):
        place = places[k]
        away = (place >= slots).astype(jnp.int32)
        hit = away * (seen == n).astype(jnp.int32)
        position = position + hit * k
        slot = slot + hit * (place - slots)
        found = found + hit
        seen = seen + away
    return position, slot, found


def count_away(places, slots):
    return sum((places[k] >= slots).astype(jnp.int32) for k in range(places.shape[0]))


def fold(block):
    total = block[:, :LANES]
    for j in range(LANES, block.shape[1], LANES):
        total = total + block[:, j : j + LANES]
    return total


def slab_terms(x, c, g, grad):
    width = grad.shape[1]
    steps = [slice(j, j + STEP) for j in range(0, width, STEP)]
    squares = sum(fold(jnp.square(x(step))) for step in steps)
    inv_rms = lax.rsqrt(jnp.sum(squares, axis=1, keepdims=True) / width + epsilon)
    inner = jnp.zeros_like(squares)
    for step in steps:
        product = x(step) * inv_rms * c(step)
        grad[:, step] += product[:8] + product[8:] if product.shape[0] == 16 else product
        inner = inner + fold(product * g[:, step].astype(jnp.float32))
    return inner


def columns(ref, rows=slice(None)):
    return lambda step: ref[:, step].astype(jnp.float32)[rows]


def choose_kernel(slots, places, far_places, store, cotangents, branch, whole, half, sem):
    mine, theirs = count_away(places, slots), count_away(far_places, slots)
    more = jnp.abs(mine - theirs)
    branch[0] = 3 * jnp.minimum(mine, theirs) + more

    @pl.when(mine > theirs)
    def _():
        pltpu.make_async_copy(cotangents.at[nth_away(places, slots, mine - 1)[0]], whole, sem).start()

    @pl.when(mine <= theirs)
    def _():
        slot = nth_away(far_places, slots, theirs - jnp.maximum(more, 1))[1]
        pltpu.make_async_copy(store.at[slot], whole, sem).start()

    pltpu.make_async_copy(store.at[0], whole, sem).wait()
    for j in range(0, whole.shape[1], STEP):
        rows = whole[:, j : j + STEP].astype(jnp.float32)
        half[:, j : j + STEP] = jnp.where(mine > theirs, rows[8:], rows[:8]).astype(half.dtype)


def choose(places, far_places, store, cotangents):
    slab = jax.ShapeDtypeStruct(store.shape[1:], store.dtype)
    half = jax.ShapeDtypeStruct((8, store.shape[2]), store.dtype)
    return pl.pallas_call(
        functools.partial(choose_kernel, store.shape[0]),
        out_shape=[jax.ShapeDtypeStruct((1,), jnp.int32), slab, half],
        in_specs=[SMEM, SMEM, HBM, HBM],
        out_specs=[SMEM, VMEM, VMEM],
        scratch_shapes=[pltpu.SemaphoreType.DMA],
        compiler_params=LIMIT,
    )(places, far_places, store, cotangents)


def pack_kernel(slots, far_places, store, out, sems):
    copies = []
    for n in range(out.shape[0]):
        slot = nth_away(far_places, slots, n)[1]
        copies.append(pltpu.make_async_copy(store.at[slot], out.at[n], sems.at[n]))
        copies[-1].start()
    for copy in copies:
        copy.wait()


def pack(far_places, store, number):
    return pl.pallas_call(
        functools.partial(pack_kernel, store.shape[0]),
        out_shape=jax.ShapeDtypeStruct((number,) + store.shape[1:], store.dtype),
        in_specs=[SMEM, HBM],
        out_specs=VMEM,
        scratch_shapes=[pltpu.SemaphoreType.DMA((number,))],
        compiler_params=LIMIT,
    )(far_places, store)


def even_kernel(slots, more, places, far_places, y, x, c, g, far_g, grad_in, inner_in, grad, inner, back, back_grad):
    mine, theirs = count_away(places, slots), count_away(far_places, slots)
    width = grad.shape[1]
    grad[...] = grad_in[...]
    back[...] = jnp.zeros_like(back)
    given = columns(y)

    @pl.when(mine > theirs)
    def _():
        rows = slice(0, y.shape[0])
        inner[...] = jnp.zeros_like(inner)
        inner[0, rows] = slab_terms(given, columns(c.at[0], rows), g, grad)

    @pl.when(mine < theirs)
    def _():
        rows = slice(x.shape[1] - y.shape[0], None)
        back_grad[...] = jnp.zeros_like(back_grad)
        sums = jnp.sum(slab_terms(columns(x.at[0], rows), given, far_g, back_grad), axis=1, keepdims=True)
        token = lax.broadcasted_iota(jnp.int32, (y.shape[0], LANES), 0) + rows.start
        lane = lax.broadcasted_iota(jnp.int32, (y.shape[0], LANES), 1)
        back[:, width:] = jnp.sum(jnp.where(token == lane, sums, 0.0), axis=0, keepdims=True)
        for j in range(0, width, STEP):
            back[:, j : j + STEP] = jnp.sum(back_grad[:, j : j + STEP], axis=0, keepdims=True)


def even_terms(places, far_places, more, y, store, cotangents, gain, far_gain, grad, inner):
    slots, slab, width = store.shape
    spare = inner.shape[0] - 1

    def own_item(places, far_places):
        mine, theirs = count_away(places, slots), count_away(far_places, slots)
        return nth_away(places, slots, mine - more)[0], mine > theirs

    def far_item(i, places, far_places):
        return nth_away(far_places, slots, count_away(far_places, slots) - 1)[1], 0, 0

    def line(i, places, far_places):
        position, ours = own_item(places, far_places)
        return jnp.where(ours, position, spare), 0, 0

    def whole(*shape):
        return pl.BlockSpec(shape, lambda i, places, far_places: (0,) * len(shape))

    return pl.pallas_call(
        functools.partial(even_kernel, slots, more),
        out_shape=(
            jax.ShapeDtypeStruct(grad.shape, grad.dtype),
            jax.ShapeDtypeStruct(inner.shape, inner.dtype),
            jax.ShapeDtypeStruct((1, width + LANES), jnp.float32),
        ),
        grid_spec=pltpu.PrefetchScalarGridSpec(
            num_scalar_prefetch=2,
            grid=(1,),
            in_specs=[
                whole(*y.shape),
                pl.BlockSpec((1, slab, width), far_item),
                pl.BlockSpec((1, slab, width), lambda i, places, far_places: (own_item(places, far_places)[0], 0, 0)),
                whole(1, width),
                whole(1, width),
                whole(8, width),
                HBM,
            ],
            out_specs=[whole(8, width), pl.BlockSpec((1, slab, LANES), line), whole(1, width + LANES)],
            scratch_shapes=[pltpu.VMEM((8, width), jnp.float32)],
        ),
        cost_estimate=pl.CostEstimate(flops=4 * 10**10, bytes_accessed=10**6, transcendentals=0),
        input_output_aliases={8: 1},
        compiler_params=LIMIT,
    )(places, far_places, y, store, cotangents, gain, far_gain, grad, inner)


def own_kernel(slots, places, x, c, g, grad, inner):
    step = pl.program_id(0)

    @pl.when(step == 0)
    def _():
        grad[...] = jnp.zeros_like(grad)

    here = places[step] < slots

    @pl.when(here)
    def _():
        inner[0] = slab_terms(columns(x.at[0]), columns(c.at[0]), g, grad)

    @pl.when(jnp.logical_not(here))
    def _():
        inner[...] = jnp.zeros_like(inner)


def own_terms(places, store, cotangents, gain):
    slots, slab, width = store.shape
    count = places.shape[0]
    return pl.pallas_call(
        functools.partial(own_kernel, slots),
        out_shape=(
            jax.ShapeDtypeStruct((8, width), jnp.float32),
            jax.ShapeDtypeStruct((count + 1, slab, LANES), jnp.float32),
        ),
        grid_spec=pltpu.PrefetchScalarGridSpec(
            num_scalar_prefetch=1,
            grid=(count,),
            in_specs=[
                pl.BlockSpec((1, slab, width), lambda i, places: (jnp.where(places[i] < slots, places[i], 0), 0, 0)),
                pl.BlockSpec((1, slab, width), lambda i, places: (i, 0, 0)),
                pl.BlockSpec((1, width), lambda i, places: (0, 0)),
            ],
            out_specs=[
                pl.BlockSpec((8, width), lambda i, places: (0, 0)),
                pl.BlockSpec((1, slab, LANES), lambda i, places: (i, 0, 0)),
            ],
        ),
        compiler_params=LIMIT,
    )(places, store, cotangents, gain)


def write_row(grad, back, row):
    for j in range(0, row.shape[1], STEP):
        row[:, j : j + STEP] = jnp.sum(grad[:, j : j + STEP], axis=0, keepdims=True) + back[:, j : j + STEP]


def far_kernel(slots, places, x, c, g, grad_in, back, inner_in, row, inner, grad):
    step = pl.program_id(0)

    @pl.when(step == 0)
    def _():
        grad[...] = grad_in[...]

    inner[0] = slab_terms(columns(x.at[0]), columns(c.at[0]), g, grad)

    @pl.when(step == pl.num_programs(0) - 1)
    def _():
        write_row(grad, back, row)


def far_terms(places, slots, x, cotangents, gain, grad, back, inner):
    number, slab, width = x.shape

    def item(i, places):
        return nth_away(places, slots, i)[0], 0, 0

    def whole(*shape):
        return pl.BlockSpec(shape, lambda i, places: (0,) * len(shape))

    return pl.pallas_call(
        functools.partial(far_kernel, slots),
        out_shape=(jax.ShapeDtypeStruct((1, width), jnp.float32), jax.ShapeDtypeStruct(inner.shape, inner.dtype)),
        grid_spec=pltpu.PrefetchScalarGridSpec(
            num_scalar_prefetch=1,
            grid=(number,),
            in_specs=[
                pl.BlockSpec((1, slab, width), lambda i, places: (i, 0, 0)),
                pl.BlockSpec((1, slab, width), item),
                whole(1, width),
                whole(8, width),
                whole(1, width + LANES),
                HBM,
            ],
            out_specs=[whole(1, width), pl.BlockSpec((1, slab, LANES), item)],
            scratch_shapes=[pltpu.VMEM((8, width), jnp.float32)],
        ),
        input_output_aliases={6: 1},
        compiler_params=LIMIT,
    )(places, x, cotangents, gain, grad, back, inner)


def gradient_row(grad, back):
    return pl.pallas_call(
        write_row,
        out_shape=jax.ShapeDtypeStruct((1, grad.shape[1]), jnp.float32),
        in_specs=[VMEM, VMEM],
        out_specs=VMEM,
    )(grad, back)


def share_over_dp(row):
    return lax.all_to_all(row.reshape(lax.axis_size("dp"), -1), "dp", 0, 0)


def whole_over_dp(shares):
    share = jnp.sum(shares, axis=0)
    return lax.all_to_all(jnp.broadcast_to(share[None], shares.shape), "dp", 0, 0).reshape(-1)


def shards(slab_store, slab_place, cotangent, norm_gain):
    store = slab_store[0, 0]
    places = slab_place[0, 0]
    slots, slab, width = store.shape
    count = places.shape[0]
    cotangents = cotangent[0, 0].reshape(count, slab, width)

    far_places = mirror(places)
    branch, whole, half = choose(places, far_places, store, cotangents)

    def exchange(fewer, more):
        def run(whole, half, cotangents):
            back = jnp.zeros((1, width + LANES), jnp.float32)
            if more:
                y = mirror(half if more == 1 else whole)
                far_gain = mirror(norm_gain)
            if fewer:
                received = mirror(pack(far_places, store, fewer))
            grad, inner = own_terms(places, store, cotangents, norm_gain)
            if more:
                grad, inner, back = even_terms(places, far_places, more, y, store, cotangents, norm_gain, far_gain, grad, inner)
                back = mirror(back)
            if fewer:
                row, inner = far_terms(places, slots, received, cotangents, norm_gain, grad, back, inner)
            else:
                row = gradient_row(grad, back)
            return row, inner, back[:, width : width + slab]

        return run

    branches = [exchange(fewer, more if fewer + more <= MOST else 0) for fewer in range(MOST + 1) for more in range(3)]
    row, inner, back = lax.switch(branch[0], branches[: 3 * MOST + 1], whole, half, cotangents)

    tokens = lax.axis_size("dp") * count * slab
    shares, places = lax.optimization_barrier((share_over_dp(row[0]), places))
    gain_grad = whole_over_dp(shares) / math.sqrt(tokens)
    away = (places >= slots).astype(jnp.int32)
    last = (away > 0) & (jnp.cumsum(away) == jnp.sum(away))
    inner_prods = jnp.sum(inner[:count], axis=-1) + jnp.where(last[:, None], back, 0.0)
    inner_prods = inner_prods.reshape(-1) / math.sqrt(width)
    return gain_grad[None, :], inner_prods[None, None, :]


def solution(mesh):
    placed = (
        P("section", "dp", None, None, None),
        P("section", "dp", None),
        P("section", "dp", None, None),
        P("section", None),
    )
    return jax.shard_map(
        shards,
        mesh=mesh,
        in_specs=placed,
        out_specs=(P("section", None), P("section", "dp", None)),
        check_vma=False,
    )
```
